128 devices in a mesh: section: 8 (over x, core), kv: 16 (over y, z).
Axes of the slice: x: 4, y: 4, z: 4, core: 2. Of those that a mesh axis runs over, the one named last changes fastest.
Arguments:
- queries: bfloat16 [1024, 8192], P(('section', 'kv')), may hold values from -72 to 72
- new_keys: bfloat16 [1024, 1024], P(('section', 'kv')), may hold values from -6 to 6
- new_values: bfloat16 [1024, 1024], P(('section', 'kv')), may hold values from -6 to 6
- prefix_keys: bfloat16 [131072, 1024], P(('section', 'kv')), may hold values from -20 to 20
- prefix_values: bfloat16 [131072, 1024], P(('section', 'kv')), may hold values from -6 to 6
- lengths: int32 [8], replicated, may hold values from 1024 to 16384, as said below
Outputs:
- attended: bfloat16 [1024, 8192], P(('section', 'kv'))
The draws below stay inside these ranges and needn't reach their ends.
Inputs may be any that keep to these rules, and one draw needn't show every extreme that they name: `lengths`: some section has 16384 live rows and another 16384 // 16.
All inputs are finite; a program needn't handle non-finite values.
Results may differ from the reference program's by a relative error of at most 0.005.
Values may be sent and summed in bfloat16 or wider, within the bound.
No kernel may reach another device: no remote copies, remote signals or barrier semaphores. Data moves between devices by JAX's collectives and lax.ppermute only.
A program may use at most 256 MiB of HBM per device.

```python
import jax
import jax.numpy as jnp
from jax import lax

H = 64
KVH = 8
DH = 128
SECTIONS = 8
QROWS = 128
PREFIX = 16384


def draw_queries(key, part):
    first = jax.random.fold_in(jax.random.fold_in(key, 17), 0)
    values = 2.5 * jnp.clip(jax.random.normal(first, (SECTIONS * QROWS, H * DH), jnp.float32), -6.0, 6.0)
    return values.astype(jnp.bfloat16)


def draw_prefix_keys(key, part):
    first = jax.random.fold_in(jax.random.fold_in(key, 23), 0)
    values = jnp.clip(jax.random.normal(first, (SECTIONS * PREFIX, KVH * DH), jnp.float32), -6.0, 6.0)
    return values.astype(jnp.bfloat16)


def draw_lengths(key, part):
    first, second = jax.random.split(jax.random.fold_in(key, 31))
    lowest = PREFIX // 16
    values = jax.random.randint(first, (SECTIONS,), lowest, PREFIX + 1, dtype=jnp.int32)
    order = jax.random.permutation(second, SECTIONS)
    values = values.at[order[0]].set(PREFIX).at[order[1]].set(lowest)
    return values


def levels(rng, extent, cuts, least, top_value):
    def one(axis_at, shards_of):
        draws = jax.random.uniform(jax.random.fold_in(jax.random.fold_in(rng, 6), axis_at), (shards_of,), jnp.float32, least / len(cuts), top_value / len(cuts))
        return jnp.repeat(jnp.exp(draws), extent[axis_at] // shards_of).reshape((-1,) + (1,) * (len(extent) - axis_at - 1))

    loudness = one(*cuts[0])
    for cut in cuts[1:]:
        loudness = loudness * one(*cut)
    return loudness


def gaussian(key, dims, width, bound, cuts=(), kind=jnp.bfloat16):
    values = width * jax.random.normal(key, dims, jnp.float32)
    if cuts:
        values = values * levels(key, dims, cuts, -0.22, 0.18)
    return jnp.clip(values, -bound, bound).astype(kind)


def setup_inputs(seed: int = 0) -> dict:
    splits = jax.random.split(jax.random.key(seed), 7)
    queries = draw_queries(jax.random.fold_in(splits[6], 71), 0)
    new_keys = gaussian(splits[1], (SECTIONS * QROWS, KVH * DH), 1.0, 6.0, ((0, 128),))
    new_values = gaussian(splits[2], (SECTIONS * QROWS, KVH * DH), 1.0, 6.0, ((0, 128),))
    prefix_keys = draw_prefix_keys(jax.random.fold_in(splits[6], 71), 0)
    prefix_values = gaussian(splits[4], (SECTIONS * PREFIX, KVH * DH), 1.0, 6.0, ((0, 128),))
    lengths = draw_lengths(jax.random.fold_in(splits[6], 71), 0)
    return dict(queries=queries, new_keys=new_keys, new_values=new_values, prefix_keys=prefix_keys, prefix_values=prefix_values, lengths=lengths)


NEG = -1.0e30


def reference(queries, new_keys, new_values, prefix_keys, prefix_values, lengths):
    group_size = H // KVH
    scale = DH ** -0.5
    pieces = []
    for section_id in range(SECTIONS):
        grouped_query_rows = queries[section_id * QROWS:(section_id + 1) * QROWS].astype(jnp.float32).reshape(QROWS, KVH, group_size, DH)
        key_rows = jnp.concatenate([prefix_keys[section_id * PREFIX:(section_id + 1) * PREFIX], new_keys[section_id * QROWS:(section_id + 1) * QROWS]], axis=0)
        value_rows = jnp.concatenate([prefix_values[section_id * PREFIX:(section_id + 1) * PREFIX], new_values[section_id * QROWS:(section_id + 1) * QROWS]], axis=0)
        key_rows = key_rows.astype(jnp.float32).reshape(PREFIX + QROWS, KVH, DH)
        value_rows = value_rows.astype(jnp.float32).reshape(PREFIX + QROWS, KVH, DH)
        places = jnp.arange(PREFIX + QROWS, dtype=jnp.int32)
        row_ids = jnp.arange(QROWS, dtype=jnp.int32)
        allowed = jnp.where(places[None, :] < PREFIX, (places < lengths[section_id])[None, :], (places[None, :] - PREFIX) <= row_ids[:, None])

        def one_head(operands):
            query_head, key_head, value_head = operands
            scores = jnp.einsum("rgd,nd->grn", query_head, key_head, precision=lax.Precision.HIGHEST) * scale
            scores = jnp.where(allowed[None], scores, NEG)
            peaks = jnp.max(scores, axis=-1, keepdims=True)
            weights = jnp.exp(scores - peaks)
            totals = jnp.sum(weights, axis=-1)
            rounded = lax.optimization_barrier(weights.astype(jnp.bfloat16)).astype(jnp.float32)
            summed = jnp.einsum("grn,nd->grd", rounded, value_head, precision=lax.Precision.HIGHEST)
            return summed / totals[..., None]

        result = lax.map(one_head, (jnp.moveaxis(grouped_query_rows, 1, 0), jnp.moveaxis(key_rows, 1, 0), jnp.moveaxis(value_rows, 1, 0)))
        pieces.append(jnp.transpose(result, (2, 0, 1, 3)).reshape(QROWS, H * DH).astype(jnp.bfloat16))
    attention = jnp.concatenate(pieces, axis=0)
    return jnp.roll(attention, QROWS, axis=0)
```

```python
import functools

import jax
import jax.numpy as jnp
from jax import lax
from jax.experimental import pallas as pl
from jax.experimental.pallas import tpu as pltpu
from jax.sharding import PartitionSpec as P

H = 64
KVH = 8
DH = 128
GROUP = H // KVH
WIDE = GROUP * DH

NEG = -1e30
FLOOR = -1e29
TINY = 1e-37
LOG2E = 1.4426950408889634
CHUNKS = 2


def attend(heads, lengths_ref, q_ref, k_ref, v_ref, nk_ref, nv_ref, o_ref, stats_ref):
    rows = q_ref.shape[0]
    keys = k_ref.shape[0]
    fresh = nk_ref.shape[0]
    step = pl.program_id(0)
    slot = lax.axis_index("kv")
    live = lengths_ref[lax.axis_index("section")] - slot * keys
    scale = DH**-0.5 * LOG2E

    @pl.when(step == 0)
    def _():
        stats_ref[...] = jnp.full(stats_ref.shape, FLOOR, jnp.float32)

    lanes = lax.broadcasted_iota(jnp.int32, (rows, DH), 1)
    own = jnp.logical_and(lanes < fresh, lanes + slot * fresh <= lax.broadcasted_iota(jnp.int32, (rows, DH), 0))
    stats_lane = lax.rem(lanes, 4 * 8)

    def padded(ref):
        blank = jnp.zeros((DH - fresh, DH), jnp.float32)
        return jnp.concatenate([ref[...].astype(jnp.float32), blank], axis=0).astype(jnp.bfloat16)

    new_k, new_v = padded(nk_ref), padded(nv_ref)
    ones = jnp.ones((DH, DH), jnp.bfloat16)
    new_v = jnp.concatenate([new_v, ones], axis=1)

    def contract(left, right, dim):
        return lax.dot_general(left, right, (((1,), (dim,)), ((), ())), preferred_element_type=jnp.float32)

    def finish(g, acc, peak):
        total = jnp.maximum(acc[:, DH:], TINY)
        o_ref[:, pl.ds(pl.multiple_of(step * WIDE + g * DH, DH), DH)] = (acc[:, :DH] / total).astype(jnp.bfloat16)
        stats_ref[...] = jnp.where(stats_lane == step * GROUP + g, peak + jnp.log2(total), stats_ref[...])

    def sweep(masked):
        k = k_ref[...]
        v = jnp.concatenate([v_ref[...], jnp.ones((keys, DH), jnp.bfloat16)], axis=1)
        allowed = lax.broadcasted_iota(jnp.int32, (1, keys), 1) < live
        for g in range(GROUP):
            q = q_ref[:, g * DH : (g + 1) * DH]
            s = contract(q, k, 1)
            if masked:
                s = jnp.where(allowed, s, NEG)
            t = jnp.where(own, contract(q, new_k, 1), NEG)
            peak = jnp.maximum(jnp.max(s, axis=1, keepdims=True), jnp.max(t, axis=1, keepdims=True))
            peak = jnp.maximum(peak * scale, FLOOR)
            w = jnp.exp2(s * scale - peak).astype(jnp.bfloat16)
            u = jnp.exp2(t * scale - peak).astype(jnp.bfloat16)
            finish(g, contract(w, v, 0) + contract(u, new_v, 0), peak)

    @pl.when(live >= keys)
    def _():
        sweep(False)

    @pl.when(jnp.logical_and(live > 0, live < keys))
    def _():
        sweep(True)

    @pl.when(live <= 0)
    def _():
        for g in range(GROUP):
            q = q_ref[:, g * DH : (g + 1) * DH]
            t = jnp.where(own, contract(q, new_k, 1), NEG)
            peak = jnp.maximum(jnp.max(t, axis=1, keepdims=True) * scale, FLOOR)
            u = jnp.exp2(t * scale - peak).astype(jnp.bfloat16)
            finish(g, contract(u, new_v, 0), peak)

    @pl.when(step == heads - 1)
    def _():
        whole = stats_ref[...]
        first = whole.astype(jnp.bfloat16)
        rest = whole - first.astype(jnp.float32)
        second = rest.astype(jnp.bfloat16)
        third = rest - second.astype(jnp.float32)
        picked = jnp.where(lanes < 32, first.astype(jnp.float32), jnp.where(lanes < 64, second.astype(jnp.float32), third))
        o_ref[:, heads * WIDE :] = picked.astype(jnp.bfloat16)


def attend_call(first, heads, lengths, q, keys, values, new_keys, new_values):
    rows, depth, fresh = q.shape[0], keys.shape[0], new_keys.shape[0]
    return pl.pallas_call(
        functools.partial(attend, heads),
        grid=(heads,),
        in_specs=[
            pl.BlockSpec(memory_space=pltpu.SMEM),
            pl.BlockSpec((rows, WIDE), lambda i: (0, i)),
            pl.BlockSpec((depth, DH), lambda i: (0, first + i)),
            pl.BlockSpec((depth, DH), lambda i: (0, first + i)),
            pl.BlockSpec((fresh, DH), lambda i: (0, first + i)),
            pl.BlockSpec((fresh, DH), lambda i: (0, first + i)),
        ],
        out_specs=pl.BlockSpec((rows, heads * WIDE + DH), lambda i: (0, 0)),
        out_shape=jax.ShapeDtypeStruct((rows, heads * WIDE + DH), jnp.bfloat16),
        scratch_shapes=[pltpu.VMEM((rows, DH), jnp.float32)],
        compiler_params=pltpu.CompilerParams(vmem_limit_bytes=32 * 1024 * 1024),
        name="attend",
    )(lengths, q, keys, values, new_keys, new_values)


def merge(heads, parts, x_ref, o_ref):
    rows = o_ref.shape[0]
    packed = x_ref[:, heads * WIDE :].astype(jnp.float32).reshape(parts, rows, DH)
    whole = packed[:, :, 0:32] + packed[:, :, 32:64] + packed[:, :, 64:96]
    peak = jnp.max(whole, axis=0, keepdims=True)
    w = jnp.exp2(whole - peak)
    w = w / jnp.sum(w, axis=0, keepdims=True)
    for h in range(heads * GROUP):
        x = x_ref[:, h * DH : (h + 1) * DH].astype(jnp.float32).reshape(parts, rows, DH)
        o_ref[:, h * DH : (h + 1) * DH] = jnp.sum(x * w[:, :, h : h + 1], axis=0).astype(jnp.bfloat16)


def merge_call(heads, parts, x):
    rows = x.shape[0] // parts
    return pl.pallas_call(
        functools.partial(merge, heads, parts),
        in_specs=[pl.BlockSpec(memory_space=pltpu.VMEM)],
        out_specs=pl.BlockSpec(memory_space=pltpu.VMEM),
        out_shape=jax.ShapeDtypeStruct((rows, heads * WIDE), jnp.bfloat16),
        compiler_params=pltpu.CompilerParams(vmem_limit_bytes=32 * 1024 * 1024),
        name="merge",
    )(x)


def on_device(queries, new_keys, new_values, prefix_keys, prefix_values, lengths):
    parts = lax.axis_size("kv")
    sections = lax.axis_size("section")
    rows = queries.shape[0]
    heads = KVH // CHUNKS
    results = []
    gathered = []
    for c in range(CHUNKS):
        own = queries[:, c * heads * WIDE : (c + 1) * heads * WIDE]
        spread = jnp.broadcast_to(own[None], (parts,) + own.shape)
        gathered.append(lax.all_to_all(spread, "kv", 0, 0, tiled=True).reshape(parts * rows, heads * WIDE))
    for c in range(CHUNKS):
        part = attend_call(c * heads, heads, lengths, gathered[c], prefix_keys, prefix_values, new_keys, new_values)
        part = lax.all_to_all(part.reshape(parts, rows, -1), "kv", 0, 0, tiled=True)
        results.append(merge_call(heads, parts, part.reshape(parts * rows, -1)))
    shift = [(s, (s + 1) % sections) for s in range(sections)]
    results = [lax.ppermute(r, "section", shift) for r in results]
    return jnp.concatenate(results, axis=1)


def solution(mesh):
    spread = P(("section", "kv"), None)
    return jax.shard_map(
        on_device,
        mesh=mesh,
        in_specs=(spread, spread, spread, spread, spread, P()),
        out_specs=spread,
        check_vma=False,
    )
```

```python
import functools

import jax
import jax.numpy as jnp
from jax import lax
from jax.experimental import pallas as pl
from jax.experimental.pallas import tpu as pltpu
from jax.sharding import PartitionSpec as P

H = 64
KVH = 8
DH = 128
GROUP = H // KVH
WIDE = GROUP * DH
SIDE = KVH // 2
AT_ONCE = 4

NEG = -1e30
FLOOR = -1e29
TINY = 1e-37
LOG2E = 1.4426950408889634
SENT = 2 * WIDE + 4 * DH
LEVELS = 2 * GROUP
STAGES = (((0, 0), (1, 0)), ((0, 1), (0, 3), (1, 1), (1, 3)), ((0, 2), (1, 2)))
MIB = 1024 * 1024
CUTS = 4


def contract(left, right, dim):
    return lax.dot_general(left, right, (((1,), (dim,)), ((), ())), preferred_element_type=jnp.float32)


def spread(q_ref, nk_ref, nv_ref, o_ref):
    rows = q_ref.shape[0]
    q, nk, nv = (ref[...].astype(jnp.float32) for ref in (q_ref, nk_ref, nv_ref))
    for pair in range(SIDE * SIDE // 2):
        both = []
        for target in (2 * pair, 2 * pair + 1):
            heads = (target % SIDE, SIDE + target // SIDE)
            pieces = [q[:, h * WIDE : (h + 1) * WIDE] for h in heads]
            pieces += [part[:, h * DH : (h + 1) * DH] for h in heads for part in (nk, nv)]
            both.append(jnp.concatenate(pieces, axis=1))
        o_ref[pair * 2 * rows : (pair + 1) * 2 * rows] = jnp.concatenate(both, axis=0).astype(jnp.bfloat16)


def spread_call(queries, new_keys, new_values):
    rows = queries.shape[0]
    return pl.pallas_call(
        spread,
        out_shape=jax.ShapeDtypeStruct((SIDE * SIDE * rows, SENT), jnp.bfloat16),
        compiler_params=pltpu.CompilerParams(vmem_limit_bytes=16 * MIB),
        name="spread",
    )(queries, new_keys, new_values)


def pack(moves, k_ref, v_ref, *refs):
    held, in_sems, out_sems = refs[-3:]
    depth = k_ref.shape[0]
    cut = depth // CUTS
    slot = lax.axis_index("kv")
    arriving = {}
    for c in range(CUTS):
        for i, ref in enumerate((k_ref, v_ref)):
            copy = pltpu.make_async_copy(ref.at[pl.ds(c * cut, cut)], held.at[i, pl.ds(c * cut, cut)], in_sems.at[2 * c + i])
            copy.start()
            arriving[c, i] = copy
    leaving = []
    for c in range(CUTS):
        for i in range(2):
            arriving[c, i].wait()
            for n, (line, step) in enumerate(moves):
                place = lax.rem(slot, SIDE) if line == 0 else lax.div(slot, SIDE)
                head = lax.rem(place + step, SIDE) + SIDE * line
                source = held.at[i, pl.ds(c * cut, cut), pl.ds(pl.multiple_of(head * DH, DH), DH)]
                target = refs[n].at[pl.ds(i * depth + c * cut, cut)]
                copy = pltpu.make_async_copy(source, target, out_sems.at[(2 * c + i) * len(moves) + n])
                copy.start()
                leaving.append(copy)
    for copy in leaving:
        copy.wait()


def pack_call(moves, keys, values):
    depth = keys.shape[0]
    return pl.pallas_call(
        functools.partial(pack, moves),
        in_specs=[pl.BlockSpec(memory_space=pl.ANY)] * 2,
        out_specs=[pl.BlockSpec(memory_space=pl.ANY)] * len(moves),
        out_shape=[jax.ShapeDtypeStruct((2 * depth, DH), jnp.bfloat16)] * len(moves),
        scratch_shapes=[
            pltpu.VMEM((2,) + keys.shape, jnp.bfloat16),
            pltpu.SemaphoreType.DMA((2 * CUTS,)),
            pltpu.SemaphoreType.DMA((2 * CUTS * len(moves),)),
        ],
        compiler_params=pltpu.CompilerParams(vmem_limit_bytes=60 * MIB),
        name="pack",
    )(keys, values)


def attend(moves, first, last, lengths_ref, q_ref, *refs):
    blocks, refs = refs[: len(moves)], refs[len(moves) :]
    rows = q_ref.shape[0]
    keys = blocks[0].shape[0] // 2
    slot = lax.axis_index("kv")
    length = lengths_ref[lax.axis_index("section")]
    place = (lax.rem(slot, SIDE), lax.div(slot, SIDE))
    scale = DH**-0.5 * LOG2E
    tall = rows * AT_ONCE
    places = lax.broadcasted_iota(jnp.int32, (1, keys), 1)
    lanes = lax.broadcasted_iota(jnp.int32, (rows, DH), 1)
    sides = []
    for line in range(2):
        mine = []
        if first:
            share = rows // SIDE
            low = place[1 - line] * share
            causal = lanes <= lax.broadcasted_iota(jnp.int32, (rows, DH), 0)
            own = jnp.logical_and(causal, jnp.logical_and(lanes >= low, lanes < low + share))
            own = jnp.concatenate([own] * AT_ONCE, axis=0)
            start = 2 * WIDE + 2 * line * DH
            mine.append((q_ref[:, start : start + DH], q_ref[:, start + DH : start + 2 * DH], own))
        for (way, step), ref in zip(moves, blocks):
            if way != line:
                continue
            back = lax.rem(place[line] + SIDE - step, SIDE)
            source = place[1] * SIDE + back if line == 0 else back * SIDE + place[0]
            mine.append((ref[:keys], ref[keys:], places < length - source * keys))
        sides.append([(k, jnp.concatenate([v, jnp.ones(v.shape, jnp.bfloat16)], axis=1), ok) for k, v, ok in mine])
    units = [(line, g, n) for line in range(2) for g in range(0, GROUP, AT_ONCE) for n in range(len(sides[line]))]

    def score(unit):
        line, g, n = unit
        columns = [q_ref[:, line * WIDE + (g + i) * DH : line * WIDE + (g + i + 1) * DH] for i in range(AT_ONCE)]
        return contract(jnp.concatenate(columns, axis=0), sides[line][n][0], 1)

    if last:
        (o_ref,) = refs if first else refs[2:]
        levels = jnp.full((rows, DH), FLOOR, jnp.float32)
    else:
        acc_out, peak_out = refs if first else refs[2:]
    s = score(units[0])
    for u, (line, g, n) in enumerate(units):
        following = score(units[u + 1]) if u + 1 < len(units) else None
        at = pl.ds((line * GROUP + g) * rows, tall)
        _, v, ok = sides[line][n]
        s = jnp.where(ok, s, NEG)
        top = jnp.broadcast_to(jnp.max(s, axis=1, keepdims=True) * scale, (tall, DH))
        if n == 0:
            old = None if first else refs[1][at]
            acc = None if first else refs[0][at]
        else:
            old = peak
        peak = jnp.maximum(top, FLOOR if old is None else old)
        w = jnp.exp2(s * scale - jnp.concatenate([peak] * (s.shape[1] // DH), axis=1)).astype(jnp.bfloat16)
        new = contract(w, v, 0)
        if old is None:
            acc = new
        else:
            factor = jnp.exp2(old - peak)
            acc = acc * jnp.concatenate([factor, factor], axis=1) + new
        if n == len(sides[line]) - 1:
            if last:
                total = jnp.maximum(acc[:, DH:], TINY)
                out = (acc[:, :DH] / total).astype(jnp.bfloat16)
                level = peak + jnp.log2(total)
                for i in range(AT_ONCE):
                    index = line * GROUP + g + i
                    o_ref[:, index * DH : (index + 1) * DH] = out[i * rows : (i + 1) * rows]
                    levels = jnp.where(lax.rem(lanes, LEVELS) == index, level[i * rows : (i + 1) * rows], levels)
            else:
                acc_out[at] = acc
                peak_out[at] = peak
        s = following
    if last:
        high = levels.astype(jnp.bfloat16).astype(jnp.float32)
        middle = (levels - high).astype(jnp.bfloat16).astype(jnp.float32)
        low = levels - high - middle
        picked = jnp.where(lanes < LEVELS, high, jnp.where(lanes < 2 * LEVELS, middle, low))
        o_ref[:, 2 * WIDE :] = picked.astype(jnp.bfloat16)


def attend_call(moves, lengths, q, blocks, state, last):
    rows = q.shape[0]
    if last:
        shapes = [jax.ShapeDtypeStruct((rows, 2 * WIDE + DH), jnp.bfloat16)]
    else:
        shapes = [jax.ShapeDtypeStruct((2 * GROUP * rows, width), jnp.float32) for width in (2 * DH, DH)]
    whole = pl.BlockSpec(memory_space=pltpu.VMEM)
    count = len(blocks) + len(state)
    return pl.pallas_call(
        functools.partial(attend, moves, not state, last),
        in_specs=[pl.BlockSpec(memory_space=pltpu.SMEM)] + [whole] * (1 + count),
        out_specs=[whole] * len(shapes),
        out_shape=shapes,
        compiler_params=pltpu.CompilerParams(vmem_limit_bytes=28 * MIB),
        name="attend",
    )(lengths, q, *blocks, *state)


def merge(x_ref, o_ref):
    rows = o_ref.shape[0]
    parts = SIDE * SIDE
    packed = x_ref[:, 2 * WIDE :].astype(jnp.float32).reshape(parts, rows, DH)
    level = packed[:, :, :LEVELS] + packed[:, :, LEVELS : 2 * LEVELS] + packed[:, :, 2 * LEVELS : 3 * LEVELS]
    level = [level[s] for s in range(parts)]
    upper = lax.broadcasted_iota(jnp.int32, (rows, LEVELS), 1) >= GROUP

    def shares(line):
        weights = [None] * parts
        for h in range(SIDE):
            group = [i * SIDE + h if line == 0 else h * SIDE + i for i in range(SIDE)]
            peak = functools.reduce(jnp.maximum, [level[s] for s in group])
            raised = [jnp.exp2(level[s] - peak) for s in group]
            total = sum(raised)
            for s, w in zip(group, raised):
                weights[s] = w / total
        return weights

    weights = [jnp.where(upper, high, low) for low, high in zip(shares(0), shares(1))]
    for line in range(2):
        for g in range(GROUP):
            index = line * GROUP + g
            x = x_ref[:, index * DH : (index + 1) * DH].astype(jnp.float32).reshape(parts, rows, DH)
            x = [x[s] * weights[s][:, index : index + 1] for s in range(parts)]
            for h in range(SIDE):
                group = [i * SIDE + h if line == 0 else h * SIDE + i for i in range(SIDE)]
                start = ((line * SIDE + h) * GROUP + g) * DH
                o_ref[:, start : start + DH] = sum(x[s] for s in group).astype(jnp.bfloat16)


def merge_call(x):
    return pl.pallas_call(
        merge,
        out_shape=jax.ShapeDtypeStruct((x.shape[0] // SIDE**2, H * DH), jnp.bfloat16),
        compiler_params=pltpu.CompilerParams(vmem_limit_bytes=16 * MIB),
        name="merge",
    )(x)


def on_device(queries, new_keys, new_values, prefix_keys, prefix_values, lengths):
    parts = lax.axis_size("kv")
    sections = lax.axis_size("section")
    rows = queries.shape[0]
    sent = spread_call(queries, new_keys, new_values)
    q = lax.all_to_all(sent.reshape(parts, rows, SENT), "kv", 0, 0, tiled=True).reshape(parts * rows, SENT)
    moves = [move for stage in STAGES for move in stage]
    far = [move for move in moves if move[1]]
    near = [move for move in moves if not move[1]]
    blocks = {}
    for move, block in zip(far + near, pack_call(far + near, prefix_keys, prefix_values)):
        line, step = move
        if step:
            pairs = []
            for a in range(SIDE):
                for b in range(SIDE):
                    to = (b + step) % SIDE
                    pairs.append((a * SIDE + b, a * SIDE + to) if line == 0 else (b * SIDE + a, to * SIDE + a))
            block = lax.ppermute(block, "kv", pairs)
        blocks[move] = block
    state = []
    for n, stage in enumerate(STAGES):
        state = attend_call(stage, lengths, q, [blocks[move] for move in stage], state, n == len(STAGES) - 1)
    part = lax.all_to_all(state[0].reshape(parts, rows, -1), "kv", 0, 0, tiled=True)
    merged = merge_call(part.reshape(parts * rows, -1))
    return lax.ppermute(merged, "section", [(s, (s + 1) % sections) for s in range(sections)])


def solution(mesh):
    split = P(("section", "kv"), None)
    return jax.shard_map(
        on_device,
        mesh=mesh,
        in_specs=(split, split, split, split, split, P()),
        out_specs=split,
        check_vma=False,
    )
```

```python
import functools

import jax
import jax.numpy as jnp
from jax import lax
from jax.experimental import pallas as pl
from jax.experimental.pallas import tpu as pltpu
from jax.sharding import PartitionSpec as P

H = 64
KVH = 8
DH = 128
GROUP = H // KVH
WIDE = GROUP * DH
SIDE = KVH // 2
AT_ONCE = 4

NEG = -1e30
FLOOR = -1e29
TINY = 1e-37
LOG2E = 1.4426950408889634
SENT = 2 * WIDE + 4 * DH
LEVELS = 2 * GROUP
STAGES = (((0, 0), (1, 0)), ((0, 1), (0, 2), (1, 1), (1, 2)), ((0, 3), (1, 3)))
MIB = 1024 * 1024
CUTS = 4


def contract(left, right, dim):
    return lax.dot_general(left, right, (((1,), (dim,)), ((), ())), preferred_element_type=jnp.float32)


def member(slot):
    return slot // SIDE % 2 * 2 + slot % 2


def partner(slot, tiling, flip):
    y, z = slot // SIDE, slot % SIDE
    y = (((y + tiling) ^ flip // 2) - tiling) % SIDE
    z = (((z + tiling) ^ flip % 2) - tiling) % SIDE
    return y * SIDE + z


def spread(q_ref, nk_ref, nv_ref, o_ref):
    rows = q_ref.shape[0]
    q, nk, nv = (ref[...].astype(jnp.float32) for ref in (q_ref, nk_ref, nv_ref))
    for pair in range(SIDE * SIDE // 2):
        both = []
        for target in (2 * pair, 2 * pair + 1):
            heads = (member(target), KVH - 1 - member(target))
            pieces = [q[:, h * WIDE : (h + 1) * WIDE] for h in heads]
            pieces += [part[:, h * DH : (h + 1) * DH] for h in heads for part in (nk, nv)]
            both.append(jnp.concatenate(pieces, axis=1))
        o_ref[pair * 2 * rows : (pair + 1) * 2 * rows] = jnp.concatenate(both, axis=0).astype(jnp.bfloat16)


def spread_call(queries, new_keys, new_values):
    rows = queries.shape[0]
    return pl.pallas_call(
        spread,
        out_shape=jax.ShapeDtypeStruct((SIDE * SIDE * rows, SENT), jnp.bfloat16),
        compiler_params=pltpu.CompilerParams(vmem_limit_bytes=60 * MIB),
        cost_estimate=pl.CostEstimate(flops=100_000_000_000, bytes_accessed=0, transcendentals=0),
        name="spread",
    )(queries, new_keys, new_values)


def pack(moves, k_ref, v_ref, *refs):
    held, in_sems, out_sems = refs[-3:]
    depth = k_ref.shape[0]
    cut = depth // CUTS
    slot = lax.axis_index("kv")
    arriving = {}
    for c in range(CUTS):
        for i, ref in enumerate((k_ref, v_ref)):
            copy = pltpu.make_async_copy(ref.at[pl.ds(c * cut, cut)], held.at[i, pl.ds(c * cut, cut)], in_sems.at[2 * c + i])
            copy.start()
            arriving[c, i] = copy
    leaving = []
    for c in range(CUTS):
        for i in range(2):
            arriving[c, i].wait()
            for n, (tiling, flip) in enumerate(moves):
                place = jnp.bitwise_xor(lax.rem(lax.div(slot, SIDE), 2) * 2 + lax.rem(slot, 2), flip)
                head = KVH - 1 - place if tiling else place
                source = held.at[i, pl.ds(c * cut, cut), pl.ds(pl.multiple_of(head * DH, DH), DH)]
                target = refs[n].at[pl.ds(i * depth + c * cut, cut)]
                copy = pltpu.make_async_copy(source, target, out_sems.at[(2 * c + i) * len(moves) + n])
                copy.start()
                leaving.append(copy)
    for copy in leaving:
        copy.wait()


def pack_call(moves, keys, values):
    depth = keys.shape[0]
    return pl.pallas_call(
        functools.partial(pack, moves),
        in_specs=[pl.BlockSpec(memory_space=pl.ANY)] * 2,
        out_specs=[pl.BlockSpec(memory_space=pl.ANY)] * len(moves),
        out_shape=[jax.ShapeDtypeStruct((2 * depth, DH), jnp.bfloat16)] * len(moves),
        scratch_shapes=[
            pltpu.VMEM((2,) + keys.shape, jnp.bfloat16),
            pltpu.SemaphoreType.DMA((2 * CUTS,)),
            pltpu.SemaphoreType.DMA((2 * CUTS * len(moves),)),
        ],
        compiler_params=pltpu.CompilerParams(vmem_limit_bytes=56 * MIB),
        name="pack",
    )(keys, values)


def attend(moves, first, last, lengths_ref, q_ref, *refs):
    blocks, refs = refs[: len(moves)], refs[len(moves) :]
    rows = q_ref.shape[0]
    keys = blocks[0].shape[0] // 2
    slot = lax.axis_index("kv")
    length = lengths_ref[lax.axis_index("section")]
    across = (lax.div(slot, SIDE), lax.rem(slot, SIDE))
    scale = DH**-0.5 * LOG2E
    tall = rows * AT_ONCE
    places = lax.broadcasted_iota(jnp.int32, (1, keys), 1)
    lanes = lax.broadcasted_iota(jnp.int32, (rows, DH), 1)
    sides = []
    for line in range(2):
        mine = []
        if first:
            share = rows // SIDE
            low = (lax.div(across[0], 2) * 2 + lax.div(across[1], 2)) * share
            causal = lanes <= lax.broadcasted_iota(jnp.int32, (rows, DH), 0)
            own = jnp.logical_and(causal, jnp.logical_and(lanes >= low, lanes < low + share))
            own = jnp.concatenate([own] * AT_ONCE, axis=0)
            start = 2 * WIDE + 2 * line * DH
            mine.append((q_ref[:, start : start + DH], q_ref[:, start + DH : start + 2 * DH], own))
        for (tiling, flip), ref in zip(moves, blocks):
            if tiling != line:
                continue
            flips = (flip // 2, flip % 2)
            y, z = (lax.rem(jnp.bitwise_xor(at + line, bit) - line + SIDE, SIDE) for at, bit in zip(across, flips))
            source = y * SIDE + z
            mine.append((ref[:keys], ref[keys:], places < length - source * keys))
        sides.append([(k, jnp.concatenate([v, jnp.ones(v.shape, jnp.bfloat16)], axis=1), ok) for k, v, ok in mine])
    units = [(line, g, n) for line in range(2) for g in range(0, GROUP, AT_ONCE) for n in range(len(sides[line]))]

    def score(unit):
        line, g, n = unit
        columns = [q_ref[:, line * WIDE + (g + i) * DH : line * WIDE + (g + i + 1) * DH] for i in range(AT_ONCE)]
        return contract(jnp.concatenate(columns, axis=0), sides[line][n][0], 1)

    if last:
        (o_ref,) = refs if first else refs[2:]
        levels = jnp.full((rows, DH), FLOOR, jnp.float32)
    else:
        acc_out, peak_out = refs if first else refs[2:]
    s = score(units[0])
    for u, (line, g, n) in enumerate(units):
        following = score(units[u + 1]) if u + 1 < len(units) else None
        at = pl.ds((line * GROUP + g) * rows, tall)
        _, v, ok = sides[line][n]
        s = jnp.where(ok, s, NEG)
        top = jnp.broadcast_to(jnp.max(s, axis=1, keepdims=True) * scale, (tall, DH))
        if n == 0:
            old = None if first else refs[1][at]
            acc = None if first else refs[0][at]
        else:
            old = peak
        peak = jnp.maximum(top, FLOOR if old is None else old)
        w = jnp.exp2(s * scale - jnp.concatenate([peak] * (s.shape[1] // DH), axis=1)).astype(jnp.bfloat16)
        new = contract(w, v, 0)
        if old is None:
            acc = new
        else:
            factor = jnp.exp2(old - peak)
            acc = acc * jnp.concatenate([factor, factor], axis=1) + new
        if n == len(sides[line]) - 1:
            if last:
                total = jnp.maximum(acc[:, DH:], TINY)
                out = (acc[:, :DH] / total).astype(jnp.bfloat16)
                level = peak + jnp.log2(total)
                for i in range(AT_ONCE):
                    index = line * GROUP + g + i
                    o_ref[:, index * DH : (index + 1) * DH] = out[i * rows : (i + 1) * rows]
                    levels = jnp.where(lax.rem(lanes, LEVELS) == index, level[i * rows : (i + 1) * rows], levels)
            else:
                acc_out[at] = acc
                peak_out[at] = peak
        s = following
    if last:
        high = levels.astype(jnp.bfloat16).astype(jnp.float32)
        middle = (levels - high).astype(jnp.bfloat16).astype(jnp.float32)
        low = levels - high - middle
        picked = jnp.where(lanes < LEVELS, high, jnp.where(lanes < 2 * LEVELS, middle, low))
        o_ref[:, 2 * WIDE :] = picked.astype(jnp.bfloat16)


def attend_call(moves, lengths, q, blocks, state, last):
    rows = q.shape[0]
    if last:
        shapes = [jax.ShapeDtypeStruct((rows, 2 * WIDE + DH), jnp.bfloat16)]
    else:
        shapes = [jax.ShapeDtypeStruct((2 * GROUP * rows, width), jnp.float32) for width in (2 * DH, DH)]
    whole = pl.BlockSpec(memory_space=pltpu.VMEM)
    count = len(blocks) + len(state)
    return pl.pallas_call(
        functools.partial(attend, moves, not state, last),
        in_specs=[pl.BlockSpec(memory_space=pltpu.SMEM)] + [whole] * (1 + count),
        out_specs=[whole] * len(shapes),
        out_shape=shapes,
        compiler_params=pltpu.CompilerParams(vmem_limit_bytes=28 * MIB),
        cost_estimate=pl.CostEstimate(flops=0, bytes_accessed=0, transcendentals=0),
        name="attend",
    )(lengths, q, *blocks, *state)


def merge(x_ref, o_ref):
    rows = o_ref.shape[0]
    parts = SIDE * SIDE
    packed = x_ref[:, 2 * WIDE :].astype(jnp.float32).reshape(parts, rows, DH)
    level = packed[:, :, :LEVELS] + packed[:, :, LEVELS : 2 * LEVELS] + packed[:, :, 2 * LEVELS : 3 * LEVELS]
    level = [level[s] for s in range(parts)]
    groups = [[s for s in range(parts) if member(s) == h] for h in range(SIDE)]
    weights = [None] * parts
    for group in groups:
        peak = functools.reduce(jnp.maximum, [level[s] for s in group])
        raised = [jnp.exp2(level[s] - peak) for s in group]
        total = sum(raised)
        for s, w in zip(group, raised):
            weights[s] = w / total
    for line in range(2):
        for g in range(GROUP):
            index = line * GROUP + g
            x = x_ref[:, index * DH : (index + 1) * DH].astype(jnp.float32).reshape(parts, rows, DH)
            x = [x[s] * weights[s][:, index : index + 1] for s in range(parts)]
            for h, group in enumerate(groups):
                start = ((KVH - 1 - h if line else h) * GROUP + g) * DH
                o_ref[:, start : start + DH] = sum(x[s] for s in group).astype(jnp.bfloat16)


def merge_call(x):
    return pl.pallas_call(
        merge,
        out_shape=jax.ShapeDtypeStruct((x.shape[0] // SIDE**2, H * DH), jnp.bfloat16),
        compiler_params=pltpu.CompilerParams(vmem_limit_bytes=16 * MIB),
        name="merge",
    )(x)


def on_device(queries, new_keys, new_values, prefix_keys, prefix_values, lengths):
    parts = lax.axis_size("kv")
    sections = lax.axis_size("section")
    rows = queries.shape[0]
    moves = [(tiling, flip) for flip in (1, 2, 3, 0) for tiling in range(2)]
    packed = dict(zip(moves, pack_call(moves, prefix_keys, prefix_values)))
    sent = spread_call(queries, new_keys, new_values)
    q = lax.all_to_all(sent.reshape(parts, rows, SENT), "kv", 0, 0, tiled=True).reshape(parts * rows, SENT)
    def travel(move, after):
        block = packed[move]
        if not move[1]:
            return block
        if after is not None:
            block = lax.optimization_barrier((block, after))[0]
        return lax.ppermute(block, "kv", [(s, partner(s, *move)) for s in range(parts)])

    blocks = {move: travel(move, None) for move in moves if move[1] != 3}
    arrived = [block for move, block in blocks.items() if move[1]]
    state = []
    for n, stage in enumerate(STAGES):
        if n == 0:
            blocks.update({move: travel(move, arrived) for move in moves if move[1] == 3})
        state = attend_call(stage, lengths, q, [blocks[move] for move in stage], state, n == len(STAGES) - 1)
    part = lax.all_to_all(state[0].reshape(parts, rows, -1), "kv", 0, 0, tiled=True)
    merged = merge_call(part.reshape(parts * rows, -1))
    return lax.ppermute(merged, "section", [(s, (s + 1) % sections) for s in range(sections)])


def solution(mesh):
    split = P(("section", "kv"), None)
    return jax.shard_map(
        on_device,
        mesh=mesh,
        in_specs=(split, split, split, split, split, P()),
        out_specs=split,
        check_vma=False,
    )
```

```python
import functools

import jax
import jax.numpy as jnp
from jax import lax
from jax.experimental import pallas as pl
from jax.experimental.pallas import tpu as pltpu
from jax.sharding import PartitionSpec as P

H = 64
KVH = 8
DH = 128
GROUP = H // KVH
WIDE = GROUP * DH
SIDE = KVH // 2
AT_ONCE = 4

NEG = -1e30
FLOOR = -1e29
TINY = 1e-37
LOG2E = 1.4426950408889634
SENT = 2 * WIDE + 4 * DH
LEVELS = 2 * GROUP
STAGES = (((0, 0), (0, 1), (0, 2), (1, 0), (1, 1), (1, 2)), ((0, 3), (1, 3)))
MIB = 1024 * 1024
CUTS = 4


def contract(left, right, dim):
    return lax.dot_general(left, right, (((1,), (dim,)), ((), ())), preferred_element_type=jnp.float32)


def member(slot):
    return slot // SIDE % 2 * 2 + slot % 2


def partner(slot, tiling, flip):
    y, z = slot // SIDE, slot % SIDE
    y = (((y + tiling) ^ flip // 2) - tiling) % SIDE
    z = (((z + tiling) ^ flip % 2) - tiling) % SIDE
    return y * SIDE + z


def spread(q_ref, nk_ref, nv_ref, o_ref):
    rows = q_ref.shape[0]
    q, nk, nv = (ref[...].astype(jnp.float32) for ref in (q_ref, nk_ref, nv_ref))
    for pair in range(SIDE * SIDE // 2):
        both = []
        for target in (2 * pair, 2 * pair + 1):
            heads = (member(target), KVH - 1 - member(target))
            pieces = [q[:, h * WIDE : (h + 1) * WIDE] for h in heads]
            pieces += [part[:, h * DH : (h + 1) * DH] for h in heads for part in (nk, nv)]
            both.append(jnp.concatenate(pieces, axis=1))
        o_ref[pair * 2 * rows : (pair + 1) * 2 * rows] = jnp.concatenate(both, axis=0).astype(jnp.bfloat16)


def spread_call(queries, new_keys, new_values):
    rows = queries.shape[0]
    return pl.pallas_call(
        spread,
        out_shape=jax.ShapeDtypeStruct((SIDE * SIDE * rows, SENT), jnp.bfloat16),
        compiler_params=pltpu.CompilerParams(vmem_limit_bytes=16 * MIB),
        cost_estimate=pl.CostEstimate(flops=100_000_000_000, bytes_accessed=0, transcendentals=0),
        name="spread",
    )(queries, new_keys, new_values)


def pack(moves, k_ref, v_ref, *refs):
    held, in_sems, out_sems = refs[-3:]
    depth = k_ref.shape[0]
    cut = depth // CUTS
    slot = lax.axis_index("kv")
    arriving = {}
    for c in range(CUTS):
        for i, ref in enumerate((k_ref, v_ref)):
            copy = pltpu.make_async_copy(ref.at[pl.ds(c * cut, cut)], held.at[i, pl.ds(c * cut, cut)], in_sems.at[2 * c + i])
            copy.start()
            arriving[c, i] = copy
    leaving = []
    for c in range(CUTS):
        for i in range(2):
            arriving[c, i].wait()
            for n, (tiling, flip) in enumerate(moves):
                place = jnp.bitwise_xor(lax.rem(lax.div(slot, SIDE), 2) * 2 + lax.rem(slot, 2), flip)
                head = KVH - 1 - place if tiling else place
                source = held.at[i, pl.ds(c * cut, cut), pl.ds(pl.multiple_of(head * DH, DH), DH)]
                target = refs[n].at[pl.ds(i * depth + c * cut, cut)]
                copy = pltpu.make_async_copy(source, target, out_sems.at[(2 * c + i) * len(moves) + n])
                copy.start()
                leaving.append(copy)
    for copy in leaving:
        copy.wait()


def pack_call(moves, keys, values):
    depth = keys.shape[0]
    return pl.pallas_call(
        functools.partial(pack, moves),
        in_specs=[pl.BlockSpec(memory_space=pl.ANY)] * 2,
        out_specs=[pl.BlockSpec(memory_space=pl.ANY)] * len(moves),
        out_shape=[jax.ShapeDtypeStruct((2 * depth, DH), jnp.bfloat16)] * len(moves),
        scratch_shapes=[
            pltpu.VMEM((2,) + keys.shape, jnp.bfloat16),
            pltpu.SemaphoreType.DMA((2 * CUTS,)),
            pltpu.SemaphoreType.DMA((2 * CUTS * len(moves),)),
        ],
        compiler_params=pltpu.CompilerParams(vmem_limit_bytes=56 * MIB),
        name="pack",
    )(keys, values)


def attend(moves, first, last, lengths_ref, q_ref, *refs):
    blocks, refs = refs[: len(moves)], refs[len(moves) :]
    rows = q_ref.shape[0]
    keys = blocks[0].shape[0] // 2
    slot = lax.axis_index("kv")
    length = lengths_ref[lax.axis_index("section")]
    across = (lax.div(slot, SIDE), lax.rem(slot, SIDE))
    scale = DH**-0.5 * LOG2E
    tall = rows * AT_ONCE
    places = lax.broadcasted_iota(jnp.int32, (1, keys), 1)
    lanes = lax.broadcasted_iota(jnp.int32, (rows, DH), 1)
    sides = []
    for line in range(2):
        mine = []
        if first:
            share = rows // SIDE
            low = (lax.div(across[0], 2) * 2 + lax.div(across[1], 2)) * share
            causal = lanes <= lax.broadcasted_iota(jnp.int32, (rows, DH), 0)
            own = jnp.logical_and(causal, jnp.logical_and(lanes >= low, lanes < low + share))
            own = jnp.concatenate([own] * AT_ONCE, axis=0)
            start = 2 * WIDE + 2 * line * DH
            mine.append((q_ref[:, start : start + DH], q_ref[:, start + DH : start + 2 * DH], own))
        for (tiling, flip), ref in zip(moves, blocks):
            if tiling != line:
                continue
            flips = (flip // 2, flip % 2)
            y, z = (lax.rem(jnp.bitwise_xor(at + line, bit) - line + SIDE, SIDE) for at, bit in zip(across, flips))
            source = y * SIDE + z
            mine.append((ref[:keys], ref[keys:], places < length - source * keys))
        k, v = (jnp.concatenate([block[i] for block in mine], axis=0) for i in range(2))
        sides.append([(k, jnp.concatenate([v, jnp.ones(v.shape, jnp.bfloat16)], axis=1), [(b[0].shape[0], b[2]) for b in mine])])
    units = [(line, g, n) for line in range(2) for g in range(0, GROUP, AT_ONCE) for n in range(len(sides[line]))]

    def score(unit):
        line, g, n = unit
        columns = [q_ref[:, line * WIDE + (g + i) * DH : line * WIDE + (g + i + 1) * DH] for i in range(AT_ONCE)]
        return contract(jnp.concatenate(columns, axis=0), sides[line][n][0], 1)

    if last:
        (o_ref,) = refs if first else refs[2:]
        levels = jnp.full((rows, DH), FLOOR, jnp.float32)
    else:
        acc_out, peak_out = refs if first else refs[2:]
    s = score(units[0])
    for u, (line, g, n) in enumerate(units):
        following = score(units[u + 1]) if u + 1 < len(units) else None
        at = pl.ds((line * GROUP + g) * rows, tall)
        _, v, masks = sides[line][n]
        pieces, start = [], 0
        for width, ok in masks:
            pieces.append(jnp.where(ok, s[:, start : start + width], NEG))
            start += width
        s = jnp.concatenate(pieces, axis=1)
        top = jnp.broadcast_to(jnp.max(s, axis=1, keepdims=True) * scale, (tall, DH))
        if n == 0:
            old = None if first else refs[1][at]
            acc = None if first else refs[0][at]
        else:
            old = peak
        peak = jnp.maximum(top, FLOOR if old is None else old)
        w = jnp.exp2(s * scale - jnp.concatenate([peak] * (s.shape[1] // DH), axis=1)).astype(jnp.bfloat16)
        new = contract(w, v, 0)
        if old is None:
            acc = new
        else:
            factor = jnp.exp2(old - peak)
            acc = acc * jnp.concatenate([factor, factor], axis=1) + new
        if n == len(sides[line]) - 1:
            if last:
                total = jnp.maximum(acc[:, DH:], TINY)
                out = (acc[:, :DH] / total).astype(jnp.bfloat16)
                level = peak + jnp.log2(total)
                for i in range(AT_ONCE):
                    index = line * GROUP + g + i
                    o_ref[:, index * DH : (index + 1) * DH] = out[i * rows : (i + 1) * rows]
                    levels = jnp.where(lax.rem(lanes, LEVELS) == index, level[i * rows : (i + 1) * rows], levels)
            else:
                acc_out[at] = acc
                peak_out[at] = peak
        s = following
    if last:
        high = levels.astype(jnp.bfloat16).astype(jnp.float32)
        middle = (levels - high).astype(jnp.bfloat16).astype(jnp.float32)
        low = levels - high - middle
        picked = jnp.where(lanes < LEVELS, high, jnp.where(lanes < 2 * LEVELS, middle, low))
        o_ref[:, 2 * WIDE :] = picked.astype(jnp.bfloat16)


def attend_call(moves, lengths, q, blocks, state, last):
    rows = q.shape[0]
    if last:
        shapes = [jax.ShapeDtypeStruct((rows, 2 * WIDE + DH), jnp.bfloat16)]
    else:
        shapes = [jax.ShapeDtypeStruct((2 * GROUP * rows, width), jnp.float32) for width in (2 * DH, DH)]
    whole = pl.BlockSpec(memory_space=pltpu.VMEM)
    count = len(blocks) + len(state)
    return pl.pallas_call(
        functools.partial(attend, moves, not state, last),
        in_specs=[pl.BlockSpec(memory_space=pltpu.SMEM)] + [whole] * (1 + count),
        out_specs=[whole] * len(shapes),
        out_shape=shapes,
        compiler_params=pltpu.CompilerParams(vmem_limit_bytes=44 * MIB),
        cost_estimate=pl.CostEstimate(flops=0, bytes_accessed=0, transcendentals=0),
        name="attend",
    )(lengths, q, *blocks, *state)


def merge(x_ref, o_ref):
    rows = o_ref.shape[0]
    parts = SIDE * SIDE
    packed = x_ref[:, 2 * WIDE :].astype(jnp.float32).reshape(parts, rows, DH)
    level = packed[:, :, :LEVELS] + packed[:, :, LEVELS : 2 * LEVELS] + packed[:, :, 2 * LEVELS : 3 * LEVELS]
    level = [level[s] for s in range(parts)]
    groups = [[s for s in range(parts) if member(s) == h] for h in range(SIDE)]
    weights = [None] * parts
    for group in groups:
        peak = functools.reduce(jnp.maximum, [level[s] for s in group])
        raised = [jnp.exp2(level[s] - peak) for s in group]
        total = sum(raised)
        for s, w in zip(group, raised):
            weights[s] = w / total
    for line in range(2):
        for g in range(GROUP):
            index = line * GROUP + g
            x = x_ref[:, index * DH : (index + 1) * DH].astype(jnp.float32).reshape(parts, rows, DH)
            x = [x[s] * weights[s][:, index : index + 1] for s in range(parts)]
            for h, group in enumerate(groups):
                start = ((KVH - 1 - h if line else h) * GROUP + g) * DH
                o_ref[:, start : start + DH] = sum(x[s] for s in group).astype(jnp.bfloat16)


def merge_call(x):
    return pl.pallas_call(
        merge,
        out_shape=jax.ShapeDtypeStruct((x.shape[0] // SIDE**2, H * DH), jnp.bfloat16),
        compiler_params=pltpu.CompilerParams(vmem_limit_bytes=16 * MIB),
        name="merge",
    )(x)


def on_device(queries, new_keys, new_values, prefix_keys, prefix_values, lengths):
    parts = lax.axis_size("kv")
    sections = lax.axis_size("section")
    rows = queries.shape[0]
    moves = [(tiling, flip) for flip in (1, 2, 3, 0) for tiling in range(2)]
    packed = dict(zip(moves, pack_call(moves, prefix_keys, prefix_values)))
    sent = spread_call(queries, new_keys, new_values)
    q = lax.all_to_all(sent.reshape(parts, rows, SENT), "kv", 0, 0, tiled=True).reshape(parts * rows, SENT)
    def travel(move, after):
        block = packed[move]
        if not move[1]:
            return block
        if after is not None:
            block = lax.optimization_barrier((block, after))[0]
        return lax.ppermute(block, "kv", [(s, partner(s, *move)) for s in range(parts)])

    blocks = {move: travel(move, None) for move in moves if move[1] != 3}
    arrived = [block for move, block in blocks.items() if move[1]]
    state = []
    for n, stage in enumerate(STAGES):
        if n == 0:
            blocks.update({move: travel(move, arrived) for move in moves if move[1] == 3})
        state = attend_call(stage, lengths, q, [blocks[move] for move in stage], state, n == len(STAGES) - 1)
    part = lax.all_to_all(state[0].reshape(parts, rows, -1), "kv", 0, 0, tiled=True)
    merged = merge_call(part.reshape(parts * rows, -1))
    return lax.ppermute(merged, "section", [(s, (s + 1) % sections) for s in range(sections)])


def solution(mesh):
    split = P(("section", "kv"), None)
    return jax.shard_map(
        on_device,
        mesh=mesh,
        in_specs=(split, split, split, split, split, P()),
        out_specs=split,
        check_vma=False,
    )
```

```python
import functools

import jax
import jax.numpy as jnp
from jax import lax
from jax.experimental import pallas as pl
from jax.experimental.pallas import tpu as pltpu
from jax.sharding import PartitionSpec as P

H = 64
KVH = 8
DH = 128
GROUP = H // KVH
WIDE = GROUP * DH
SIDE = KVH // 2
AT_ONCE = 4

NEG = -1e30
FLOOR = -1e29
TINY = 1e-37
LOG2E = 1.4426950408889634
SENT = 2 * WIDE + 4 * DH
LEVELS = 2 * GROUP
STAGES = (((0, 0), (0, 1), (0, 2), (1, 0), (1, 1), (1, 2)), ((0, 3), (1, 3)))
MIB = 1024 * 1024
CUTS = 2


def contract(left, right, dim):
    return lax.dot_general(left, right, (((1,), (dim,)), ((), ())), preferred_element_type=jnp.float32)


def member(slot):
    return slot // SIDE % 2 * 2 + slot % 2


def partner(slot, tiling, flip):
    y, z = slot // SIDE, slot % SIDE
    y = (((y + tiling) ^ flip // 2) - tiling) % SIDE
    z = (((z + tiling) ^ flip % 2) - tiling) % SIDE
    return y * SIDE + z


def spread(q_ref, nk_ref, nv_ref, o_ref):
    rows = q_ref.shape[0]
    q, nk, nv = (ref[...].astype(jnp.float32) for ref in (q_ref, nk_ref, nv_ref))
    for pair in range(SIDE * SIDE // 2):
        both = []
        for target in (2 * pair, 2 * pair + 1):
            heads = (member(target), KVH - 1 - member(target))
            pieces = [q[:, h * WIDE : (h + 1) * WIDE] for h in heads]
            pieces += [part[:, h * DH : (h + 1) * DH] for h in heads for part in (nk, nv)]
            both.append(jnp.concatenate(pieces, axis=1))
        o_ref[pair * 2 * rows : (pair + 1) * 2 * rows] = jnp.concatenate(both, axis=0).astype(jnp.bfloat16)


def spread_call(queries, new_keys, new_values):
    rows = queries.shape[0]
    return pl.pallas_call(
        spread,
        out_shape=jax.ShapeDtypeStruct((SIDE * SIDE * rows, SENT), jnp.bfloat16),
        compiler_params=pltpu.CompilerParams(vmem_limit_bytes=16 * MIB),
        cost_estimate=pl.CostEstimate(flops=100_000_000_000, bytes_accessed=0, transcendentals=0),
        name="spread",
    )(queries, new_keys, new_values)


def pack(moves, k_ref, v_ref, *refs):
    held, in_sems, out_sems = refs[-3:]
    depth = k_ref.shape[0]
    cut = depth // CUTS
    slot = lax.axis_index("kv")
    arriving = {}
    for c in range(CUTS):
        for i, ref in enumerate((k_ref, v_ref)):
            copy = pltpu.make_async_copy(ref.at[pl.ds(c * cut, cut)], held.at[i, pl.ds(c * cut, cut)], in_sems.at[2 * c + i])
            copy.start()
            arriving[c, i] = copy
    leaving = []
    for c in range(CUTS):
        for i in range(2):
            arriving[c, i].wait()
            for n, (tiling, flip) in enumerate(moves):
                place = jnp.bitwise_xor(lax.rem(lax.div(slot, SIDE), 2) * 2 + lax.rem(slot, 2), flip)
                head = KVH - 1 - place if tiling else place
                source = held.at[i, pl.ds(c * cut, cut), pl.ds(pl.multiple_of(head * DH, DH), DH)]
                target = refs[n].at[pl.ds(i * depth + c * cut, cut)]
                copy = pltpu.make_async_copy(source, target, out_sems.at[(2 * c + i) * len(moves) + n])
                copy.start()
                leaving.append(copy)
    for copy in leaving:
        copy.wait()


def pack_call(moves, keys, values):
    depth = keys.shape[0]
    return pl.pallas_call(
        functools.partial(pack, moves),
        in_specs=[pl.BlockSpec(memory_space=pl.ANY)] * 2,
        out_specs=[pl.BlockSpec(memory_space=pl.ANY)] * len(moves),
        out_shape=[jax.ShapeDtypeStruct((2 * depth, DH), jnp.bfloat16)] * len(moves),
        scratch_shapes=[
            pltpu.VMEM((2,) + keys.shape, jnp.bfloat16),
            pltpu.SemaphoreType.DMA((2 * CUTS,)),
            pltpu.SemaphoreType.DMA((2 * CUTS * len(moves),)),
        ],
        compiler_params=pltpu.CompilerParams(vmem_limit_bytes=56 * MIB),
        name="pack",
    )(keys, values)


def attend(moves, first, last, lengths_ref, q_ref, *refs):
    blocks, refs = refs[: len(moves)], refs[len(moves) :]
    rows = q_ref.shape[0]
    keys = blocks[0].shape[0] // 2
    slot = lax.axis_index("kv")
    length = lengths_ref[lax.axis_index("section")]
    across = (lax.div(slot, SIDE), lax.rem(slot, SIDE))
    scale = DH**-0.5 * LOG2E
    tall = rows * AT_ONCE
    places = lax.broadcasted_iota(jnp.int32, (1, keys), 1)
    lanes = lax.broadcasted_iota(jnp.int32, (rows, DH), 1)
    sides = []
    for line in range(2):
        mine = []
        if first:
            share = rows // SIDE
            low = (lax.div(across[0], 2) * 2 + lax.div(across[1], 2)) * share
            causal = lanes <= lax.broadcasted_iota(jnp.int32, (rows, DH), 0)
            own = jnp.logical_and(causal, jnp.logical_and(lanes >= low, lanes < low + share))
            own = jnp.concatenate([own] * AT_ONCE, axis=0)
            start = 2 * WIDE + 2 * line * DH
            mine.append((q_ref[:, start : start + DH], q_ref[:, start + DH : start + 2 * DH], own))
        for (tiling, flip), ref in zip(moves, blocks):
            if tiling != line:
                continue
            flips = (flip // 2, flip % 2)
            y, z = (lax.rem(jnp.bitwise_xor(at + line, bit) - line + SIDE, SIDE) for at, bit in zip(across, flips))
            source = y * SIDE + z
            mine.append((ref[:keys], ref[keys:], places < length - source * keys))
        k, v = (jnp.concatenate([block[i] for block in mine], axis=0) for i in range(2))
        sides.append([(k, jnp.concatenate([v, jnp.ones(v.shape, jnp.bfloat16)], axis=1), [(b[0].shape[0], b[2]) for b in mine])])
    units = [(line, g, n) for line in range(2) for g in range(0, GROUP, AT_ONCE) for n in range(len(sides[line]))]

    def score(unit):
        line, g, n = unit
        columns = [q_ref[:, line * WIDE + (g + i) * DH : line * WIDE + (g + i + 1) * DH] for i in range(AT_ONCE)]
        return contract(jnp.concatenate(columns, axis=0), sides[line][n][0], 1)

    if last:
        (o_ref,) = refs if first else refs[2:]
        levels = jnp.full((rows, DH), FLOOR, jnp.float32)
    else:
        acc_out, peak_out = refs if first else refs[2:]
    s = score(units[0])
    for u, (line, g, n) in enumerate(units):
        following = score(units[u + 1]) if u + 1 < len(units) else None
        at = pl.ds((line * GROUP + g) * rows, tall)
        _, v, masks = sides[line][n]
        pieces, start = [], 0
        for width, ok in masks:
            pieces.append(jnp.where(ok, s[:, start : start + width], NEG))
            start += width
        s = jnp.concatenate(pieces, axis=1)
        top = jnp.broadcast_to(jnp.max(s, axis=1, keepdims=True) * scale, (tall, DH))
        if n == 0:
            old = None if first else refs[1][at]
            acc = None if first else refs[0][at]
        else:
            old = peak
        peak = jnp.maximum(top, FLOOR if old is None else old)
        w = jnp.exp2(s * scale - jnp.concatenate([peak] * (s.shape[1] // DH), axis=1)).astype(jnp.bfloat16)
        new = contract(w, v, 0)
        if old is None:
            acc = new
        else:
            factor = jnp.exp2(old - peak)
            acc = acc * jnp.concatenate([factor, factor], axis=1) + new
        if n == len(sides[line]) - 1:
            if last:
                total = jnp.maximum(acc[:, DH:], TINY)
                out = (acc[:, :DH] / total).astype(jnp.bfloat16)
                level = peak + jnp.log2(total)
                for i in range(AT_ONCE):
                    index = line * GROUP + g + i
                    o_ref[:, index * DH : (index + 1) * DH] = out[i * rows : (i + 1) * rows]
                    levels = jnp.where(lax.rem(lanes, LEVELS) == index, level[i * rows : (i + 1) * rows], levels)
            else:
                acc_out[at] = acc
                peak_out[at] = peak
        s = following
    if last:
        high = levels.astype(jnp.bfloat16).astype(jnp.float32)
        middle = (levels - high).astype(jnp.bfloat16).astype(jnp.float32)
        low = levels - high - middle
        picked = jnp.where(lanes < LEVELS, high, jnp.where(lanes < 2 * LEVELS, middle, low))
        o_ref[:, 2 * WIDE :] = picked.astype(jnp.bfloat16)


def attend_call(moves, lengths, q, blocks, state, last):
    rows = q.shape[0]
    if last:
        shapes = [jax.ShapeDtypeStruct((rows, 2 * WIDE + DH), jnp.bfloat16)]
    else:
        shapes = [jax.ShapeDtypeStruct((2 * GROUP * rows, width), jnp.float32) for width in (2 * DH, DH)]
    whole = pl.BlockSpec(memory_space=pltpu.VMEM)
    count = len(blocks) + len(state)
    return pl.pallas_call(
        functools.partial(attend, moves, not state, last),
        in_specs=[pl.BlockSpec(memory_space=pltpu.SMEM)] + [whole] * (1 + count),
        out_specs=[whole] * len(shapes),
        out_shape=shapes,
        compiler_params=pltpu.CompilerParams(vmem_limit_bytes=44 * MIB),
        cost_estimate=pl.CostEstimate(flops=0, bytes_accessed=0, transcendentals=0),
        name="attend",
    )(lengths, q, *blocks, *state)


def merge(x_ref, o_ref):
    rows = o_ref.shape[0]
    parts = SIDE * SIDE
    packed = x_ref[:, 2 * WIDE :].astype(jnp.float32).reshape(parts, rows, DH)
    level = packed[:, :, :LEVELS] + packed[:, :, LEVELS : 2 * LEVELS] + packed[:, :, 2 * LEVELS : 3 * LEVELS]
    level = [level[s] for s in range(parts)]
    groups = [[s for s in range(parts) if member(s) == h] for h in range(SIDE)]
    weights = [None] * parts
    for group in groups:
        peak = functools.reduce(jnp.maximum, [level[s] for s in group])
        raised = [jnp.exp2(level[s] - peak) for s in group]
        total = sum(raised)
        for s, w in zip(group, raised):
            weights[s] = w / total
    for line in range(2):
        for g in range(GROUP):
            index = line * GROUP + g
            x = x_ref[:, index * DH : (index + 1) * DH].astype(jnp.float32).reshape(parts, rows, DH)
            x = [x[s] * weights[s][:, index : index + 1] for s in range(parts)]
            for h, group in enumerate(groups):
                start = ((KVH - 1 - h if line else h) * GROUP + g) * DH
                o_ref[:, start : start + DH] = sum(x[s] for s in group).astype(jnp.bfloat16)


def merge_call(x):
    return pl.pallas_call(
        merge,
        out_shape=jax.ShapeDtypeStruct((x.shape[0] // SIDE**2, H * DH), jnp.bfloat16),
        compiler_params=pltpu.CompilerParams(vmem_limit_bytes=16 * MIB),
        name="merge",
    )(x)


def on_device(queries, new_keys, new_values, prefix_keys, prefix_values, lengths):
    parts = lax.axis_size("kv")
    sections = lax.axis_size("section")
    rows = queries.shape[0]
    moves = [(tiling, flip) for flip in (1, 2, 3, 0) for tiling in range(2)]
    packed = dict(zip(moves, pack_call(moves, prefix_keys, prefix_values)))
    sent = spread_call(queries, new_keys, new_values)
    q = lax.all_to_all(sent.reshape(parts, rows, SENT), "kv", 0, 0, tiled=True).reshape(parts * rows, SENT)
    def travel(move, after):
        block = packed[move]
        if not move[1]:
            return block
        if after is not None:
            block = lax.optimization_barrier((block, after))[0]
        return lax.ppermute(block, "kv", [(s, partner(s, *move)) for s in range(parts)])

    blocks = {move: travel(move, None) for move in moves if move[1] != 3}
    arrived = [block for move, block in blocks.items() if move[1]]
    state = []
    for n, stage in enumerate(STAGES):
        if n == 0:
            blocks.update({move: travel(move, arrived) for move in moves if move[1] == 3})
        state = attend_call(stage, lengths, q, [blocks[move] for move in stage], state, n == len(STAGES) - 1)
    part = lax.all_to_all(state[0].reshape(parts, rows, -1), "kv", 0, 0, tiled=True)
    merged = merge_call(part.reshape(parts * rows, -1))
    return lax.ppermute(merged, "section", [(s, (s + 1) % sections) for s in range(sections)])


def solution(mesh):
    split = P(("section", "kv"), None)
    return jax.shard_map(
        on_device,
        mesh=mesh,
        in_specs=(split, split, split, split, split, P()),
        out_specs=split,
        check_vma=False,
    )
```
